32 devices in a mesh: groups: 2 (over x), row: 16 (over z, y, core).
Axes of the slice: x: 2, y: 2, z: 4, core: 2. Of those that a mesh axis runs over, the one named last changes fastest.
Arguments:
- tile_values: bfloat16 [4096, 128, 128], P(('groups', 'row')), parts along dimension 0, may hold values from -6 to 6
- tile_rows: int32 [4096], P(('groups', 'row')), parts along dimension 0, may hold values from 0 to 63
- tile_cols: int32 [4096], P(('groups', 'row')), parts along dimension 0, may hold values from 0 to 2047, as said below
- tile_exps: int32 [4096], P(('groups', 'row')), parts along dimension 0, may hold values from 0 to 4
- sketch_matrix: bfloat16 [262144, 256], P('row'), may hold values from -6 to 6
Outputs:
- basis_rows: float32 [262144, 256], P(('groups', 'row')), parts along dimension 0
- range_factor: float32 [512, 256], P('groups'), parts along dimension 0
The draws below stay inside these ranges and needn't reach their ends.
There are 2 independent parts, one for each index of `groups`. The reference program is written for one: setup_inputs(seed, part) draws one part's arguments, and reference() takes and returns one part's arrays. A program takes and returns all parts, laid end to end along the dimension named above; an argument that names none is the same for every part. Nothing has to cross between parts.
Inputs may be any that keep to these rules, and one draw needn't show every extreme that they name: `tile_cols`: entry t of the list of one index of row (t from 0 to 127) names a column block from (t // 8) * 128 to (t // 8 + 1) * 128 - 1, so that the rows of sketch_matrix it needs lie on index t // 8 of row.
All inputs are finite; a program needn't handle non-finite values.
Results may differ from the reference program's by a relative error of at most 0.0003.
Values may be sent and summed in bfloat16 or wider, within the bound.
No kernel may reach another device: no remote copies, remote signals or barrier semaphores. Data moves between devices by JAX's collectives and lax.ppermute only.
A program may use at most 128 MiB of HBM per device.

```python
import math
import jax
import jax.numpy as jnp
from jax import lax

NCOL = 262144
K = 256
TILE = 128
RB_DEV = 64
TILES_DEV = 128
SLOTS = 8
CBLK = 2048
CPO = 128
ROWS_DEV = 8192
ROWS = 131072
TILES = 2048
N_ROW = 16


def draw_tile_cols(key, part):
    position = jnp.arange(TILES, dtype=jnp.int32) % TILES_DEV
    holder = position // SLOTS
    offset = jax.random.randint(jax.random.fold_in(key, 11), (TILES,), 0, CPO, dtype=jnp.int32)
    return holder * CPO + offset


def draw_tile_exps(key, part):
    device_of = jnp.arange(TILES, dtype=jnp.int32) // TILES_DEV
    rising = 3 * device_of // N_ROW
    own_level = jax.random.randint(jax.random.fold_in(key, 31), (TILES,), 0, 3, dtype=jnp.int32)
    return own_level + rising


def draw_sketch_matrix(key, part):
    common_key = jax.random.fold_in(key, 21)
    own_key = jax.random.fold_in(key, 22)
    column_key = jax.random.fold_in(key, 23)
    common = jax.random.truncated_normal(common_key, -4.0, 4.0, (NCOL, 1), jnp.float32)
    own_part = jax.random.truncated_normal(own_key, -4.0, 4.0, (NCOL, K), jnp.float32)
    lowest = 1.0 / 4.0
    weight_common = 0.3
    column_level = jnp.exp(jax.random.uniform(column_key, (K,), jnp.float32) * math.log(lowest))
    mixed = weight_common * common + column_level[None, :] * own_part
    return (mixed / jnp.sqrt(weight_common * weight_common + column_level * column_level)[None, :]).astype(jnp.bfloat16)


def plant(entries, rng, least, largest):
    longest = entries.shape.index(max(entries.shape))
    spots = []
    for shift in (0, 1):
        where = [jax.random.randint(jax.random.fold_in(rng, axis), (), 0, length) for axis, length in enumerate(entries.shape)]
        where[longest] = (where[longest] + shift) % entries.shape[longest]
        spots.append(tuple(where))
    return entries.at[spots[0]].set(least).at[spots[1]].set(largest)


def block_levels(rng, dims, cuts, least, high):
    def one(dim, shards_of):
        steps = jax.random.uniform(jax.random.fold_in(jax.random.fold_in(rng, 6), dim), (shards_of,), jnp.float32, least / len(cuts), high / len(cuts))
        return jnp.repeat(jnp.exp(steps), dims[dim] // shards_of).reshape((-1,) + (1,) * (len(dims) - dim - 1))

    level = one(*cuts[0])
    for cut in cuts[1:]:
        level = level * one(*cut)
    return level


def normal_values(rng, shape, scale, most, split=(), kind=jnp.bfloat16):
    entries = scale * jax.random.normal(rng, shape, jnp.float32)
    if split:
        entries = entries * block_levels(rng, shape, split, -0.22, 0.18)
    return jnp.clip(entries, -most, most).astype(kind)


def setup_inputs(seed: int = 0, part: int = 0) -> dict:
    key_list = jax.random.split(jax.random.key(seed), 6)
    part_keys = jax.random.split(jax.random.fold_in(key_list[5], part), 6)
    return {
        "tile_values": normal_values(part_keys[0], (TILES, TILE, TILE), 1.0, 6.0, ((0, 16),)),
        "tile_rows": plant(jax.random.randint(part_keys[1], (TILES,), 0, RB_DEV), jax.random.fold_in(part_keys[1], 1), 0, RB_DEV - 1).astype(jnp.int32),
        "tile_cols": draw_tile_cols(jax.random.fold_in(jax.random.fold_in(key_list[5], part), 71), part),
        "tile_exps": draw_tile_exps(jax.random.fold_in(jax.random.fold_in(key_list[5], part), 71), part),
        "sketch_matrix": draw_sketch_matrix(jax.random.fold_in(key_list[5], 71), part),
    }


def reference(tile_values, tile_rows, tile_cols, tile_exps, sketch_matrix):
    col_blocks = sketch_matrix.reshape(CBLK, TILE, K)

    def one_shard(shard_args):
        shard_tiles, shard_rows, shard_cols, shard_exps = shard_args
        fetched = col_blocks[shard_cols].astype(jnp.float32)
        products = jnp.einsum('tij,tjc->tic', shard_tiles.astype(jnp.float32), fetched, precision=lax.Precision.HIGHEST)
        tile_scale = jnp.exp2(shard_exps.astype(jnp.float32))
        placing = jnp.where(jnp.arange(RB_DEV, dtype=jnp.int32)[:, None] == shard_rows[None, :], tile_scale[None, :], jnp.zeros((), jnp.float32))
        summed = jnp.dot(placing, products.reshape(TILES_DEV, TILE * K), precision=lax.Precision.HIGHEST)
        return summed.reshape(ROWS_DEV, K)
    sketch = lax.map(one_shard, (tile_values.reshape(N_ROW, TILES_DEV, TILE, TILE), tile_rows.reshape(N_ROW, TILES_DEV), tile_cols.reshape(N_ROW, TILES_DEV), tile_exps.reshape(N_ROW, TILES_DEV)))
    sketch = sketch.reshape(ROWS, K)
    q_factor, r_factor = jnp.linalg.qr(sketch)
    diag_signs = jnp.sign(jnp.diagonal(r_factor))
    root_rows = math.sqrt(ROWS)
    basis_rows = q_factor * diag_signs[None, :] * root_rows
    range_factor = r_factor * diag_signs[:, None] / root_rows
    return (basis_rows, range_factor)
```

```python
import functools
import math

import jax
import jax.numpy as jnp
from jax import lax
from jax.experimental import pallas as pl
from jax.experimental.pallas import tpu as pltpu
from jax.sharding import PartitionSpec as P

RB_DEV = 64
PANEL = 32
HIGHEST = lax.Precision.HIGHEST


def split_bf16(value):
    high = value.astype(jnp.bfloat16)
    low = (value - high.astype(jnp.float32)).astype(jnp.bfloat16)
    return high, low


def dot_f32(left, right, contract):
    return lax.dot_general(
        left, right, (contract, ((), ())), preferred_element_type=jnp.float32
    )


def gather_kernel(index_ref, blocks_ref, found_ref, sem):
    count = found_ref.shape[0]

    @pl.loop(0, count)
    def _(at):
        pltpu.make_async_copy(
            blocks_ref.at[index_ref[at]], found_ref.at[at], sem
        ).start()

    pltpu.make_async_copy(found_ref, found_ref, sem).wait()


def gather_blocks(indices, col_blocks):
    count = indices.shape[0]
    return pl.pallas_call(
        gather_kernel,
        grid_spec=pltpu.PrefetchScalarGridSpec(
            num_scalar_prefetch=1,
            grid=(1,),
            in_specs=[pl.BlockSpec(memory_space=pl.ANY)],
            out_specs=pl.BlockSpec(memory_space=pl.ANY),
            scratch_shapes=[pltpu.SemaphoreType.DMA],
        ),
        out_shape=jax.ShapeDtypeStruct((count,) + col_blocks.shape[1:], col_blocks.dtype),
        name="gather_blocks",
    )(indices, col_blocks)


def sketch_kernel(
    rows_ref, exps_ref, tiles_ref, fetched_ref, sketch_ref, gram_ref, total, sem
):
    step = pl.program_id(0)
    chunk, tile_size, _ = tiles_ref.shape

    @pl.when(step == 0)
    def _():
        total[...] = jnp.zeros_like(total)

    for t in range(chunk):
        at = step * chunk + t
        row = rows_ref[at]
        scale = (jnp.int32(1) << exps_ref[at]).astype(jnp.float32)
        product = jnp.dot(tiles_ref[t], fetched_ref[t], preferred_element_type=jnp.float32)
        total[row] += product * scale

    @pl.when(step == pl.num_programs(0) - 1)
    def _():
        copy = pltpu.make_async_copy(total, sketch_ref, sem)
        copy.start()
        gram_ref[...] = jnp.zeros_like(gram_ref)

        @pl.loop(0, total.shape[0] // 4)
        def _(i):
            block = total[pl.ds(i * 4, 4)].reshape(4 * tile_size, total.shape[2])
            h, l = split_bf16(block)
            over_rows = ((0,), (0,))
            cross = dot_f32(h, l, over_rows)
            gram_ref[...] += dot_f32(h, h, over_rows) + dot_f32(l, l, over_rows) + (cross + cross.T)

        copy.wait()


def sketch_and_gram(tile_rows, tile_exps, tile_values, fetched, chunk):
    count, tile_size, _ = tile_values.shape
    width = fetched.shape[2]
    return pl.pallas_call(
        sketch_kernel,
        grid_spec=pltpu.PrefetchScalarGridSpec(
            num_scalar_prefetch=2,
            grid=(count // chunk,),
            in_specs=[
                pl.BlockSpec((chunk, tile_size, tile_size), lambda i, r, e: (i, 0, 0)),
                pl.BlockSpec((chunk, tile_size, width), lambda i, r, e: (i, 0, 0)),
            ],
            out_specs=[
                pl.BlockSpec(memory_space=pl.ANY),
                pl.BlockSpec((width, width), lambda i, r, e: (0, 0)),
            ],
            scratch_shapes=[
                pltpu.VMEM((RB_DEV, tile_size, width), jnp.float32),
                pltpu.SemaphoreType.DMA,
            ],
        ),
        out_shape=[
            jax.ShapeDtypeStruct((RB_DEV, tile_size, width), jnp.float32),
            jax.ShapeDtypeStruct((width, width), jnp.float32),
        ],
        compiler_params=pltpu.CompilerParams(vmem_limit_bytes=40 * 2**20),
        name="sketch_and_gram",
    )(tile_rows, tile_exps, tile_values, fetched)


def eliminate_block(block):
    size = block.shape[0]
    at_row = lax.broadcasted_iota(jnp.int32, block.shape, 0)
    for k in range(size):
        inverse = lax.rsqrt(block[k : k + 1, k : k + 1])
        row = block[k : k + 1, :] * inverse
        column = block[:, k : k + 1] * inverse
        below = jnp.where(at_row > k, block - column * row, block)
        block = jnp.where(at_row == k, jnp.broadcast_to(row, block.shape), below)
    return block


def factor(work, width):
    for start in range(0, width, PANEL):
        end = start + PANEL
        eye = (
            lax.broadcasted_iota(jnp.int32, (PANEL, PANEL), 0)
            == lax.broadcasted_iota(jnp.int32, (PANEL, PANEL), 1)
        ).astype(jnp.float32)
        diagonal = work[start:end, start:end]
        solved = eliminate_block(jnp.concatenate([diagonal, eye], axis=1))
        lower_inverse = solved[:, PANEL:]
        panel = jnp.dot(
            lower_inverse, work[start:end, :], precision=HIGHEST, preferred_element_type=jnp.float32
        )
        work[start:end, :] = panel
        if end < width:
            work[end:width, :] -= lax.dot_general(
                panel[:, end:width],
                panel,
                (((0,), (0,)), ((), ())),
                precision=HIGHEST,
                preferred_element_type=jnp.float32,
            )


def basis_kernel(root_rows, gram_ref, sketch_ref, basis_ref, range_ref, work, inv_high, inv_low):
    width = gram_ref.shape[0]

    @pl.when(pl.program_id(0) == 0)
    def _():
        work[:, :width] = gram_ref[...]
        rows = lax.broadcasted_iota(jnp.int32, (width, width), 0)
        cols = lax.broadcasted_iota(jnp.int32, (width, width), 1)
        work[:, width:] = (rows == cols).astype(jnp.float32)
        factor(work, width)
        range_ref[...] = jnp.where(rows <= cols, work[:, :width] / root_rows, 0.0)
        lower = jnp.where(rows >= cols, work[:, width:] * root_rows, 0.0)
        h, l = split_bf16(lower)
        inv_high[...] = h
        inv_low[...] = l

    h, l = split_bf16(sketch_ref[...])
    over_columns = ((1,), (1,))
    basis_ref[...] = (
        dot_f32(h, inv_high[...], over_columns)
        + dot_f32(h, inv_low[...], over_columns)
        + dot_f32(l, inv_high[...], over_columns)
    )


def basis_and_range(gram, sketch, root_rows, chunk):
    rows, width = sketch.shape
    return pl.pallas_call(
        functools.partial(basis_kernel, root_rows),
        grid=(rows // chunk,),
        in_specs=[
            pl.BlockSpec((width, width), lambda i: (0, 0)),
            pl.BlockSpec((chunk, width), lambda i: (i, 0)),
        ],
        out_specs=[
            pl.BlockSpec((chunk, width), lambda i: (i, 0)),
            pl.BlockSpec((width, width), lambda i: (0, 0)),
        ],
        out_shape=[
            jax.ShapeDtypeStruct((rows, width), jnp.float32),
            jax.ShapeDtypeStruct((width, width), jnp.float32),
        ],
        scratch_shapes=[
            pltpu.VMEM((width, 2 * width), jnp.float32),
            pltpu.VMEM((width, width), jnp.bfloat16),
            pltpu.VMEM((width, width), jnp.bfloat16),
        ],
        compiler_params=pltpu.CompilerParams(vmem_limit_bytes=40 * 2**20),
        name="basis_and_range",
    )(gram, sketch)


def sum_over_row(part):
    devices = lax.axis_size("row")
    if devices & (devices - 1):
        return lax.psum(part, "row")
    hop = 1
    while hop < devices:
        part = part + lax.ppermute(part, "row", [(i, i ^ hop) for i in range(devices)])
        hop *= 2
    return part


def on_device(tile_values, tile_rows, tile_cols, tile_exps, sketch_matrix):
    row_devices = lax.axis_size("row")
    tile_count, tile_size, _ = tile_values.shape
    width = sketch_matrix.shape[1]
    owned_blocks = sketch_matrix.shape[0] // tile_size
    slot_count = tile_count // row_devices
    col_blocks = sketch_matrix.reshape(owned_blocks, tile_size, width)
    local_block = (tile_cols % owned_blocks).reshape(row_devices, slot_count)
    wanted = lax.all_to_all(local_block, "row", split_axis=0, concat_axis=0, tiled=True)
    found = gather_blocks(wanted.reshape(tile_count), col_blocks)
    found = found.reshape(row_devices, slot_count, tile_size, width)
    fetched = lax.all_to_all(found, "row", split_axis=0, concat_axis=0, tiled=True)
    fetched = fetched.reshape(tile_count, tile_size, width)
    sketch, gram = sketch_and_gram(tile_rows, tile_exps, tile_values, fetched, 16)
    sketch = sketch.reshape(RB_DEV * tile_size, width)
    root_rows = math.sqrt(sketch.shape[0] * row_devices)
    return tuple(basis_and_range(sum_over_row(gram), sketch, root_rows, 1024))


def solution(mesh):
    return jax.shard_map(
        on_device,
        mesh=mesh,
        in_specs=(
            P(("groups", "row"), None, None),
            P(("groups", "row")),
            P(("groups", "row")),
            P(("groups", "row")),
            P("row", None),
        ),
        out_specs=(P(("groups", "row"), None), P("groups", None)),
        check_vma=False,
    )
```

```python
import functools
import math

import jax
import jax.numpy as jnp
from jax import lax
from jax.experimental import pallas as pl
from jax.experimental.pallas import tpu as pltpu
from jax.sharding import PartitionSpec as P

RB_DEV = 64
PANEL = 64
PIVOTS = 8
GRAM_BLOCKS = 8
LATE_PART = (0, 4)
VMEM_LIMIT = 56 * 2**20
HIGHEST = lax.Precision.HIGHEST


def split_bf16(value):
    high = value.astype(jnp.bfloat16)
    low = (value - high.astype(jnp.float32)).astype(jnp.bfloat16)
    return high, low


def dot_f32(left, right, contract):
    return lax.dot_general(
        left, right, (contract, ((), ())), preferred_element_type=jnp.float32
    )


def gather_kernel(first, index_ref, blocks_ref, found_ref, held, in_sems, out_sem):
    devices, slots = found_ref.shape[:2]
    owned_blocks = blocks_ref.shape[0]
    for d in range(devices):
        for s in range(slots):
            block = lax.rem(index_ref[d, 0, first + s], owned_blocks)
            pltpu.make_async_copy(blocks_ref.at[block], held.at[d, s], in_sems.at[d]).start()
    for d in range(devices):
        pltpu.make_async_copy(held.at[d], held.at[d], in_sems.at[d]).wait()
        pltpu.make_async_copy(held.at[d], found_ref.at[d], out_sem).start()
    pltpu.make_async_copy(held, found_ref, out_sem).wait()


def gather_blocks(wanted, col_blocks, first, slots):
    shape = (wanted.shape[0], slots) + col_blocks.shape[1:]
    return pl.pallas_call(
        functools.partial(gather_kernel, first),
        in_specs=[
            pl.BlockSpec(memory_space=pltpu.SMEM),
            pl.BlockSpec(memory_space=pl.ANY),
        ],
        out_specs=pl.BlockSpec(memory_space=pl.ANY),
        out_shape=jax.ShapeDtypeStruct(shape, col_blocks.dtype),
        scratch_shapes=[
            pltpu.VMEM(shape, col_blocks.dtype),
            pltpu.SemaphoreType.DMA((shape[0],)),
            pltpu.SemaphoreType.DMA,
        ],
        compiler_params=pltpu.CompilerParams(vmem_limit_bytes=VMEM_LIMIT),
        cost_estimate=pl.CostEstimate(
            flops=0, bytes_accessed=2 * 2 * math.prod(shape), transcendentals=0
        ),
        name="gather_blocks",
    )(wanted, col_blocks)


def add_products(first, slot_count, rows_ref, exps_ref, tiles_ref, fetched_ref, total):
    devices, slots = tiles_ref.shape[:2]
    for d in range(devices):
        for s in range(slots):
            at = (pl.program_id(0) * devices + d) * slot_count + first + s
            scale = (jnp.int32(1) << exps_ref[at]).astype(jnp.float32)
            tile = (tiles_ref[d, s].astype(jnp.float32) * scale).astype(jnp.bfloat16)
            total[rows_ref[at]] += jnp.dot(
                tile, fetched_ref[d, s], preferred_element_type=jnp.float32
            )


def early_kernel(first, slot_count, rows_ref, exps_ref, tiles_ref, fetched_ref, sketch_ref, total, sem):
    @pl.when(pl.program_id(0) == 0)
    def _():
        total[...] = jnp.zeros_like(total)

    add_products(first, slot_count, rows_ref, exps_ref, tiles_ref, fetched_ref, total)

    @pl.when(pl.program_id(0) == pl.num_programs(0) - 1)
    def _():
        copy = pltpu.make_async_copy(total, sketch_ref, sem)
        copy.start()
        copy.wait()


def late_kernel(
    first, slot_count, has_early, rows_ref, exps_ref, tiles_ref, fetched_ref, *refs
):
    if has_early:
        early_ref, sketch_ref, gram_ref, total, sem, early, early_sem = refs
    else:
        sketch_ref, gram_ref, total, sem = refs

    @pl.when(pl.program_id(0) == 0)
    def _():
        if has_early:
            pltpu.make_async_copy(early_ref, early, early_sem).start()
        total[...] = jnp.zeros_like(total)

    add_products(first, slot_count, rows_ref, exps_ref, tiles_ref, fetched_ref, total)

    @pl.when(pl.program_id(0) == pl.num_programs(0) - 1)
    def _():
        blocks, tile_size, width = total.shape
        gram_ref[...] = jnp.zeros_like(gram_ref)
        if has_early:
            pltpu.make_async_copy(early_ref, early, early_sem).wait()

        @pl.loop(0, blocks // GRAM_BLOCKS)
        def _(i):
            part = pl.ds(i * GRAM_BLOCKS, GRAM_BLOCKS)
            block = total[part]
            if has_early:
                block = block + early[part]
                total[part] = block
            pltpu.make_async_copy(total.at[part], sketch_ref.at[part], sem).start()
            h, l = split_bf16(block.reshape(GRAM_BLOCKS * tile_size, width))
            over_rows = ((0,), (0,))
            for at, (rows, cols) in enumerate(upper_blocks(width)):
                gram_ref[at] += (
                    dot_f32(h[:, rows], h[:, cols], over_rows)
                    + dot_f32(h[:, rows], l[:, cols], over_rows)
                    + dot_f32(l[:, rows], h[:, cols], over_rows)
                    + dot_f32(l[:, rows], l[:, cols], over_rows)
                )

        pltpu.make_async_copy(total, sketch_ref, sem).wait()


def upper_blocks(width):
    half = width // 2
    left, right = slice(0, half), slice(half, width)
    return (left, left), (left, right), (right, right)


def sketch_part(tile_rows, tile_exps, tile_values, fetched, first, early, last):
    devices, slot_count, tile_size, _ = tile_values.shape
    slots, width = fetched.shape[1], fetched.shape[3]
    steps = devices
    while steps % 2 == 0 and devices * slots < 24 * steps:
        steps //= 2
    group = devices // steps
    place = lambda i, r, e: (i, first // slots, 0, 0)
    sketch_shape = (RB_DEV, tile_size, width)
    inputs = [tile_rows, tile_exps, tile_values, fetched]
    in_specs = [
        pl.BlockSpec((group, slots, tile_size, tile_size), place),
        pl.BlockSpec((group, slots, tile_size, width), lambda i, r, e: (i, 0, 0, 0)),
    ]
    out_specs = [pl.BlockSpec(memory_space=pl.ANY)]
    out_shape = [jax.ShapeDtypeStruct(sketch_shape, jnp.float32)]
    scratch = [pltpu.VMEM(sketch_shape, jnp.float32), pltpu.SemaphoreType.DMA]
    kernel = functools.partial(early_kernel, first, slot_count)
    if last:
        kernel = functools.partial(late_kernel, first, slot_count, early is not None)
        out_specs.append(pl.BlockSpec((3, width // 2, width // 2), lambda i, r, e: (0, 0, 0)))
        out_shape.append(jax.ShapeDtypeStruct((3, width // 2, width // 2), jnp.float32))
        if early is not None:
            inputs.append(early)
            in_specs.append(pl.BlockSpec(memory_space=pl.ANY))
            scratch += [pltpu.VMEM(sketch_shape, jnp.float32), pltpu.SemaphoreType.DMA]
    tiles = devices * slots
    return pl.pallas_call(
        kernel,
        grid_spec=pltpu.PrefetchScalarGridSpec(
            num_scalar_prefetch=2,
            grid=(steps,),
            in_specs=in_specs,
            out_specs=out_specs,
            scratch_shapes=scratch,
        ),
        out_shape=out_shape,
        compiler_params=pltpu.CompilerParams(vmem_limit_bytes=VMEM_LIMIT),
        cost_estimate=pl.CostEstimate(
            flops=2 * tiles * tile_size * tile_size * width,
            bytes_accessed=2 * tiles * tile_size * (tile_size + width) + 4 * math.prod(sketch_shape),
            transcendentals=0,
        ),
        name="late_sketch" if last else "early_sketch",
    )(*inputs)


def eliminate_block(block):
    size, lanes = block.shape
    done = []
    for start in range(0, size, PIVOTS):
        shape = (size - start, lanes)
        at_row = lax.broadcasted_iota(jnp.int32, shape, 0)
        columns = [
            jnp.broadcast_to(block[:, start + j : start + j + 1], shape) for j in range(PIVOTS)
        ]
        scale = jnp.zeros((PIVOTS, lanes), jnp.float32)
        for i in range(PIVOTS):
            pivot = columns[i][i : i + 1, :]
            factors = jnp.where(at_row > i, columns[i] * (1.0 / pivot), 0.0)
            for j in range(i + 1, PIVOTS):
                columns[j] = columns[j] - factors * columns[j][i : i + 1, :]
            block = block - factors * block[i : i + 1, :]
            scale = jnp.where(at_row[:PIVOTS] == i, lax.rsqrt(pivot), scale)
        done.append(block[:PIVOTS] * scale)
        block = block[PIVOTS:]
    return jnp.concatenate(done, axis=0)


def factor(work, width):
    for start in range(0, width, PANEL):
        end = start + PANEL
        eye = (
            lax.broadcasted_iota(jnp.int32, (PANEL, PANEL), 0)
            == lax.broadcasted_iota(jnp.int32, (PANEL, PANEL), 1)
        ).astype(jnp.float32)
        diagonal = work[start:end, start:end]
        solved = eliminate_block(jnp.concatenate([diagonal, eye], axis=1))
        lower_inverse = solved[:, PANEL:]
        panel = jnp.dot(
            lower_inverse, work[start:end, :], precision=HIGHEST, preferred_element_type=jnp.float32
        )
        work[start:end, :] = panel
        if end < width:
            work[end:width, :] -= lax.dot_general(
                panel[:, end:width],
                panel,
                (((0,), (0,)), ((), ())),
                precision=HIGHEST,
                preferred_element_type=jnp.float32,
            )


def basis_kernel(root_rows, order_ref, own_ref, other_ref, sketch_ref, basis_ref, range_ref, work, inv_high, inv_low):
    width = range_ref.shape[0]

    @pl.when(pl.program_id(0) == 0)
    def _():
        own, other = own_ref[...], other_ref[...]
        swapped = order_ref[0] == 1
        both = jnp.concatenate(
            [jnp.where(swapped, other, own), jnp.where(swapped, own, other)], axis=0
        ).reshape(3, width // 2, width // 2)
        for at, (rows, cols) in enumerate(upper_blocks(width)):
            work[rows, cols] = both[at]
        left, right = slice(0, width // 2), slice(width // 2, width)
        work[right, left] = both[1].T
        rows = lax.broadcasted_iota(jnp.int32, (width, width), 0)
        cols = lax.broadcasted_iota(jnp.int32, (width, width), 1)
        work[:, width:] = (rows == cols).astype(jnp.float32)
        factor(work, width)
        range_ref[...] = jnp.where(rows <= cols, work[:, :width] * (1.0 / root_rows), 0.0)
        lower = jnp.where(rows >= cols, work[:, width:] * root_rows, 0.0)
        h, l = split_bf16(lower)
        inv_high[...] = h
        inv_low[...] = l

    h, l = split_bf16(sketch_ref[...])
    over_columns = ((1,), (1,))
    basis_ref[...] = (
        dot_f32(h, inv_high[...], over_columns)
        + dot_f32(h, inv_low[...], over_columns)
        + dot_f32(l, inv_high[...], over_columns)
    )


def basis_and_range(order, own, other, sketch, root_rows, chunk):
    rows, width = sketch.shape
    half_spec = pl.BlockSpec(own.shape, lambda i, o: (0, 0))
    return pl.pallas_call(
        functools.partial(basis_kernel, root_rows),
        grid_spec=pltpu.PrefetchScalarGridSpec(
            num_scalar_prefetch=1,
            grid=(rows // chunk,),
            in_specs=[half_spec, half_spec, pl.BlockSpec((chunk, width), lambda i, o: (i, 0))],
            out_specs=[
                pl.BlockSpec((chunk, width), lambda i, o: (i, 0)),
                pl.BlockSpec((width, width), lambda i, o: (0, 0)),
            ],
            scratch_shapes=[
                pltpu.VMEM((width, 2 * width), jnp.float32),
                pltpu.VMEM((width, width), jnp.bfloat16),
                pltpu.VMEM((width, width), jnp.bfloat16),
            ],
        ),
        out_shape=[
            jax.ShapeDtypeStruct((rows, width), jnp.float32),
            jax.ShapeDtypeStruct((width, width), jnp.float32),
        ],
        compiler_params=pltpu.CompilerParams(vmem_limit_bytes=VMEM_LIMIT),
        name="basis_and_range",
    )(order, own, other, sketch)


def swap(value, hop):
    devices = lax.axis_size("row")
    return lax.ppermute(value, "row", [(i, i ^ hop) for i in range(devices)])


def sum_over_row(gram):
    devices = lax.axis_size("row")
    gram = gram.reshape(-1, gram.shape[-1])
    half = gram.shape[0] // 2
    if devices & (devices - 1) or devices == 1:
        gram = lax.psum(gram, "row")
        return jnp.zeros((1,), jnp.int32), gram[:half], gram[half:]
    side = lax.axis_index("row") % 2
    own = lax.dynamic_slice_in_dim(gram, side * half, half, 0)
    other = lax.dynamic_slice_in_dim(gram, (1 - side) * half, half, 0)
    own = own + swap(other, 1)
    hop = 2
    while hop < devices:
        own = own + swap(own, hop)
        hop *= 2
    return side.reshape(1).astype(jnp.int32), own, swap(own, 1)


def on_device(tile_values, tile_rows, tile_cols, tile_exps, sketch_matrix):
    row_devices = lax.axis_size("row")
    tile_count, tile_size, _ = tile_values.shape
    width = sketch_matrix.shape[1]
    slot_count = tile_count // row_devices
    col_blocks = sketch_matrix.reshape(-1, tile_size, width)
    tiles = tile_values.reshape(row_devices, slot_count, tile_size, tile_size)
    wanted = lax.all_to_all(
        tile_cols.reshape(row_devices, 1, slot_count), "row", split_axis=0, concat_axis=0, tiled=True
    )
    late = slot_count * LATE_PART[0] // LATE_PART[1]
    parts = [(0, slot_count - late), (slot_count - late, late)] if late else [(0, slot_count)]
    fetched = []
    for first, slots in parts:
        found = gather_blocks(wanted, col_blocks, first, slots)
        fetched.append(lax.all_to_all(found, "row", split_axis=0, concat_axis=0, tiled=True))
    early = None
    if late:
        [early] = sketch_part(tile_rows, tile_exps, tiles, fetched[0], 0, None, False)
    sketch, gram = sketch_part(tile_rows, tile_exps, tiles, fetched[-1], parts[-1][0], early, True)
    sketch = sketch.reshape(RB_DEV * tile_size, width)
    root_rows = math.sqrt(sketch.shape[0] * row_devices)
    return tuple(basis_and_range(*sum_over_row(gram), sketch, root_rows, 1024))


def solution(mesh):
    return jax.shard_map(
        on_device,
        mesh=mesh,
        in_specs=(
            P(("groups", "row"), None, None),
            P(("groups", "row")),
            P(("groups", "row")),
            P(("groups", "row")),
            P("row", None),
        ),
        out_specs=(P(("groups", "row"), None), P("groups", None)),
        check_vma=False,
    )
```
